32 devices in a mesh: groups: 2 (over x), gx: 8 (over z, y), gy: 2 (over core).
Axes of the slice: x: 2, y: 2, z: 4, core: 2. Of those that a mesh axis runs over, the one named last changes fastest.
Arguments:
- plume_state: bfloat16 [4, 20, 32, 256, 128], P('groups', None, 'gx', 'gy'), parts along dimension 0, may hold values from -6 to 6
- spectral_weight: bfloat16 [2, 128, 24, 800], P('gy', 'gx'), may hold values from -8 to 8
- pointwise_weight: bfloat16 [20, 20], replicated, may hold values from -1.25 to 1.25
- channel_bias: float32 [20], replicated, may hold values from -3 to 3
Outputs:
- next_state: bfloat16 [4, 20, 32, 256, 128], P('groups', None, 'gx', 'gy'), parts along dimension 0
The draws below stay inside these ranges and needn't reach their ends.
There are 2 independent parts, one for each index of `groups`. The reference program is written for one: setup_inputs(seed, part) draws one part's arguments, and reference() takes and returns one part's arrays. A program takes and returns all parts, laid end to end along the dimension named above; an argument that names none is the same for every part. Nothing has to cross between parts.
All inputs are finite; a program needn't handle non-finite values.
Results may differ from the reference program's by a relative error of at most 0.014.
Values may be sent and summed in bfloat16 or wider, within the bound.
A program may use at most 128 MiB of HBM per device.

```python
import math
import jax
import jax.numpy as jnp
from jax import lax

TS = 2
C = 20
CX = 4
CY = 128
NZ = 128
MX = 24
MY = 16
MZ = 16
NX = 32
NY = 256
PAIR_GY = 128
N_GX = 8
N_GY = 2


def block_scale(rng, extent, split, low, largest):
    def one(axis_at, blocks):
        draws = jax.random.uniform(jax.random.fold_in(jax.random.fold_in(rng, 6), axis_at), (blocks,), jnp.float32, low / len(split), largest / len(split))
        return jnp.repeat(jnp.exp(draws), extent[axis_at] // blocks).reshape((-1,) + (1,) * (len(extent) - axis_at - 1))

    level = one(*split[0])
    for cut in split[1:]:
        level = level * one(*cut)
    return level


def centred(stream_key, dims, deviation, reach, cuts=(), kind=jnp.bfloat16):
    result = jax.random.normal(stream_key, dims, jnp.float32) * deviation
    if len(cuts) > 0:
        result = block_scale(stream_key, dims, cuts, -0.22, 0.18) * result
    return jnp.clip(result, min=-reach, max=reach).astype(kind)


def setup_inputs(seed: int = 0, part: int = 0) -> dict:
    key_of = jax.random.split(jax.random.key(seed), 5)
    own_keys = jax.random.split(jax.random.fold_in(key_of[4], part), 5)
    plume_state = centred(own_keys[0], (TS, C, NX, NY, NZ), 1.0, 6.0, ((2, 8), (3, 2)))
    spectral_weight = centred(key_of[1], (N_GY, PAIR_GY, MX, 2 * C * C), (max(1, (CX * N_GX * CY * N_GY * NZ) // (4 * C * MX * MY * MZ)) ** 0.5), 8.0, ((0, 2), (1, 8)))
    pointwise_weight = centred(key_of[2], (C, C), C ** -0.5, 1.25)
    channel_bias = centred(key_of[3], (C,), 0.5, 3.0, (), jnp.float32)
    return {"plume_state": plume_state, "spectral_weight": spectral_weight, "pointwise_weight": pointwise_weight, "channel_bias": channel_bias}


def retained(kept, length):
    indices = jnp.arange(kept, dtype=jnp.int32)
    return jnp.where(indices < kept // 2, indices, length - kept + indices).astype(jnp.int32)


def phases(freq_ids, positions, length):
    product = (freq_ids[:, None] * positions[None, :]) % length
    return (2.0 * math.pi / length) * product.astype(jnp.float32)


def forward_table(freq_ids, positions, length):
    angles = phases(freq_ids, positions, length).T
    cosine = jnp.cos(angles)
    sine_part = jnp.sin(angles)
    stacked = jnp.stack([jnp.stack([cosine, -sine_part], 1), jnp.stack([sine_part, cosine], 1)], 1)
    return stacked.astype(jnp.bfloat16)


def inverse_table(freq_ids, positions, length):
    angles = phases(freq_ids, positions, length)
    cosine = jnp.cos(angles)
    sine_part = jnp.sin(angles)
    stacked = jnp.stack([jnp.stack([cosine, sine_part], 1), jnp.stack([-sine_part, cosine], 1)], 0)
    return stacked.astype(jnp.bfloat16)


def depth_tables(depth):
    angles = phases(jnp.arange(MZ, dtype=jnp.int32), jnp.arange(depth, dtype=jnp.int32), depth)
    cosine = jnp.cos(angles)
    sine_part = jnp.sin(angles)
    forward = jnp.concatenate([cosine.T, -sine_part.T], 1).astype(jnp.bfloat16)
    doubling = jnp.where(jnp.arange(MZ) == 0, 1.0, 2.0).astype(jnp.float32)[:, None]
    inverse = jnp.stack([doubling * cosine, -doubling * sine_part], 0).astype(jnp.bfloat16)
    return forward, inverse


def rounded(values):
    return lax.optimization_barrier(values.astype(jnp.bfloat16)).astype(jnp.float32)


def reference(plume_state, spectral_weight, pointwise_weight, channel_bias):
    z_forward, z_inverse = depth_tables(NZ)
    z_forward = z_forward.astype(jnp.float32)
    z_inverse = z_inverse.astype(jnp.float32)
    y_forward = forward_table(retained(MY, NY), jnp.arange(NY, dtype=jnp.int32), NY).astype(jnp.float32)
    x_forward = forward_table(retained(MX, NX), jnp.arange(NX, dtype=jnp.int32), NX).astype(jnp.float32)
    y_inverse = inverse_table(retained(MY, NY), jnp.arange(NY, dtype=jnp.int32), NY).astype(jnp.float32)
    x_inverse = inverse_table(retained(MX, NX), jnp.arange(NX, dtype=jnp.int32), NX).astype(jnp.float32)
    spectral = spectral_weight.astype(jnp.float32).reshape(MY * MZ, MX, 2, C, C)
    weight_real = spectral[:, :, 0]
    weight_imag = spectral[:, :, 1]
    pointwise = pointwise_weight.astype(jnp.float32)
    inverse_size = 1.0 / (NX * NY * NZ)

    def one_step(snapshot):
        fields = snapshot.astype(jnp.float32)
        depth_modes = rounded(jnp.einsum('cxyz,zk->cxky', fields, z_forward)).reshape(C, NX, 2, MZ, NY)
        row_modes = rounded(jnp.einsum('cxpky,ypqm->cxqkm', depth_modes, y_forward)).reshape(C, NX, 2, MY * MZ)
        pair_modes = rounded(jnp.einsum('cxpf,xpqk->fcqk', row_modes, x_forward))
        mode_real = pair_modes[:, :, 0]
        mode_imag = pair_modes[:, :, 1]
        mixed_real = jnp.einsum('fck,fkcd->fdk', mode_real, weight_real) - jnp.einsum('fck,fkcd->fdk', mode_imag, weight_imag)
        mixed_imag = jnp.einsum('fck,fkcd->fdk', mode_real, weight_imag) + jnp.einsum('fck,fkcd->fdk', mode_imag, weight_real)
        mixed_modes = rounded(jnp.stack([mixed_real, mixed_imag], 2))
        cells_x = rounded(jnp.einsum('fdqk,qkpx->dxpf', mixed_modes, x_inverse)).reshape(C, NX, 2, MZ, MY)
        cells_y = rounded(jnp.einsum('dxqkm,qmpy->dxpky', cells_x, y_inverse))
        spectral_part = jnp.einsum('dxpky,pkz->dxyz', cells_y, z_inverse) * inverse_size
        pointwise_part = jnp.einsum('cxyz,cd->dxyz', fields, pointwise) + channel_bias[:, None, None, None]
        return jax.nn.gelu(spectral_part + pointwise_part, approximate=False).astype(jnp.bfloat16)

    return lax.map(one_step, plume_state)
```

```python
import functools
import math

import jax
import jax.numpy as jnp
import ml_dtypes
import numpy as np
from jax import lax
from jax.experimental import pallas as pl
from jax.experimental.pallas import tpu as pltpu
from jax.sharding import PartitionSpec as P

MX = 24
MY = 16
MZ = 16
LANES = 128
TILE = 16
MESH = pl.DeviceIdType.MESH
F32 = jnp.float32
BF16 = jnp.bfloat16


def retained(kept, length):
    indices = np.arange(kept)
    return np.where(indices < kept // 2, indices, length - kept + indices)


def phases(freq_ids, positions, length):
    product = freq_ids[:, None] * positions[None, :] % length
    return np.float32(2.0 * math.pi / length) * product.astype(np.float32)


def forward_table(freq_ids, positions, length):
    angles = phases(freq_ids, positions, length).T
    cosine, sine = np.cos(angles), np.sin(angles)
    return np.stack([np.stack([cosine, -sine], 1), np.stack([sine, cosine], 1)], 1)


def inverse_table(freq_ids, positions, length):
    angles = phases(freq_ids, positions, length)
    cosine, sine = np.cos(angles), np.sin(angles)
    return np.stack([np.stack([cosine, sine], 1), np.stack([-sine, cosine], 1)], 0)


def up(value, step):
    return -(-value // step) * step


def pad_last(table, width):
    return np.pad(table, [(0, 0)] * (table.ndim - 1) + [(0, width - table.shape[-1])])


def tables(n_gx, n_gy, rows_x, rows_y, depth, pair_rows, group):
    length_x, length_y = n_gx * rows_x, n_gy * rows_y
    blocks = MY // pair_rows
    lanes_l = up(pair_rows * MX, LANES)
    angles = phases(np.arange(MZ), np.arange(depth), depth)
    z_forward = np.concatenate([np.cos(angles), -np.sin(angles)], 0)

    y_ids, x_ids = retained(MY, length_y), retained(MX, length_x)
    eye_x, eye_m = np.eye(rows_x), np.eye(pair_rows)
    fy = forward_table(y_ids, np.arange(length_y), length_y)
    fy = fy.reshape(n_gy, rows_y, 2, 2, blocks, pair_rows)
    y_forward = np.einsum("gypqbm,xw->gpxybwqm", fy, eye_x)
    y_forward = y_forward.reshape(n_gy, 2 * rows_x * rows_y, blocks, -1)
    y_forward = pad_last(y_forward, LANES).reshape(n_gy, 2 * rows_x * rows_y, blocks * LANES)

    fx = forward_table(x_ids, np.arange(length_x), length_x).reshape(n_gx, rows_x, 2, 2, MX)
    x_forward = np.einsum("ixqpk,mn->pnkixqm", fx, eye_m).reshape(2, pair_rows * MX, n_gx, -1)
    x_forward = pad_last(x_forward, LANES).reshape(2, pair_rows * MX, n_gx * LANES)
    x_forward = np.pad(x_forward, [(0, 0), (0, lanes_l - pair_rows * MX), (0, 0)])
    x_forward = x_forward.reshape(2 * lanes_l, n_gx * LANES).T

    ix = inverse_table(x_ids, np.arange(length_x), length_x).reshape(2, MX, 2, n_gx, rows_x)
    x_back = np.einsum("qkpix,mn->qnkixpm", ix, eye_m).reshape(2, pair_rows * MX, n_gx, -1)
    x_back = pad_last(x_back, LANES).reshape(2, pair_rows * MX, n_gx * LANES)
    x_back = np.pad(x_back, [(0, 0), (0, lanes_l - pair_rows * MX), (0, 0)])
    x_back = x_back.reshape(2 * lanes_l, n_gx * LANES)

    iy = inverse_table(y_ids, np.arange(length_y), length_y)
    iy = iy.reshape(2, blocks, pair_rows, 2, n_gy, rows_y)
    y_back = np.einsum("qbmpgy,xw->gxpybwqm", iy, eye_x)
    y_back = y_back.reshape(n_gy, rows_x, 2 * rows_y, blocks, -1)
    y_back = pad_last(y_back, LANES).reshape(n_gy, rows_x, 2 * rows_y, blocks * LANES)

    doubling = np.where(np.arange(MZ) == 0, 1.0, 2.0)[:, None]
    iz = np.stack([doubling * np.cos(angles), -doubling * np.sin(angles)], 0)
    iz = iz.astype(ml_dtypes.bfloat16).astype(np.float32) / (length_x * length_y * depth)
    z_back = np.einsum("pkz,jh->pjkhz", iz, np.eye(group))
    z_back = z_back.reshape(2 * group * MZ, group * depth)
    return [
        jnp.asarray(np.ascontiguousarray(t, dtype=np.float32).astype(ml_dtypes.bfloat16))
        for t in (z_forward, y_forward, x_forward, x_back, y_back, z_back)
    ]


def dot(a, b):
    return jnp.dot(a, b, preferred_element_type=F32)


def dot_lanes(a, b):
    return lax.dot_general(a, b, (((1,), (1,)), ((), ())), preferred_element_type=F32)


def forward_kernel(fields, steps, plume, z_forward, y_forward, out, rows):
    step = pl.program_id(0)
    half = lax.axis_index("gy")
    group = plume.shape[0]
    blocks = y_forward.shape[2] // LANES
    parts = []
    for j in range(group):
        modes = dot_lanes(z_forward[...], plume[j]).astype(BF16)
        parts.append(jnp.concatenate([modes[:MZ], modes[MZ:]], axis=1))
    terms = dot(jnp.concatenate(parts, axis=0), y_forward[half])
    size = group * MZ
    for block in range(blocks):
        rows[block, pl.ds(pl.multiple_of(step * size, size), size), :] = terms[
            :, block * LANES : (block + 1) * LANES
        ]

    @pl.when(step == steps - 1)
    def _():
        slot_rows = out.shape[1]
        if slot_rows > fields:
            extra = (slot_rows - fields) * MZ
            rows[:, pl.ds(fields * MZ, extra), :] = jnp.zeros((blocks, extra, LANES), F32)
        for kz in range(MZ):
            for block in range(blocks):
                out[kz * blocks + block] = rows[
                    block, pl.ds(kz, slot_rows, stride=MZ), :
                ].astype(BF16)


def each(count, one):
    if count <= 16:
        for s in range(1, count):
            one(s)
    else:
        lax.fori_loop(1, count, lambda s, _: (one(s), 0)[1], 0)


def modes_kernel(
    n_gx, n_gy, snapshots, channels,
    sent, weights, x_forward, x_back, out,
    landed, back, going, mixers, pairs, mixed, order,
    send_one, recv_one, send_two, recv_two,
):
    count = n_gx * n_gy
    my_x, my_y = lax.axis_index("gx"), lax.axis_index("gy")
    me = my_y * n_gx + my_x
    fields = snapshots * channels
    wide = mixers.shape[1]

    def device(index):
        return {"gx": lax.rem(index, n_gx), "gy": lax.div(index, n_gx)}

    barrier = pltpu.get_barrier_semaphore()

    def greet(s):
        peer = lax.rem(me + s, count)
        pl.semaphore_signal(barrier, inc=1, device_id=device(peer), device_id_type=MESH)

    each(count, greet)
    pl.semaphore_wait(barrier, count - 1)

    def first(s, at):
        peer = lax.rem(me + s, count)
        return pltpu.make_async_remote_copy(
            src_ref=sent.at[peer], dst_ref=landed.at[at],
            send_sem=send_one.at[s], recv_sem=recv_one.at[s],
            device_id=device(peer), device_id_type=MESH,
        )

    def second(s, at):
        peer = lax.rem(me + s, count)
        return pltpu.make_async_remote_copy(
            src_ref=going.at[lax.rem(peer, n_gx)], dst_ref=back.at[at],
            send_sem=send_two.at[s], recv_sem=recv_two.at[s],
            device_id=device(peer), device_id_type=MESH,
        )

    def source(s):
        return lax.rem(me + count - s, count)

    each(count, lambda s: first(s, me).start())
    landed[me] = sent[me]

    length = weights.shape[1]
    for at in range(0, length, LANES):
        width = min(LANES, length - at)
        chunk = weights[:, pl.ds(at, width)].astype(F32)
        if width < LANES:
            chunk = jnp.concatenate([chunk, jnp.zeros((wide, LANES - width), F32)], axis=1)
        mixers[pl.ds(at, LANES), :] = chunk.T

    each(count, lambda s: first(s, source(s)).wait_recv())
    summed = []
    for i in range(n_gx):
        total = landed[i].astype(F32)
        for g in range(1, n_gy):
            total += landed[g * n_gx + i].astype(F32)
        summed.append(total.astype(BF16))
    pairs[...] = dot(jnp.concatenate(summed, axis=1), x_forward[...]).astype(BF16).astype(F32)

    square = channels * channels
    mixed[...] = jnp.zeros_like(mixed)
    for t in range(snapshots):
        real = jnp.zeros((channels, wide), F32)
        imag = jnp.zeros((channels, wide), F32)
        for c in range(channels):
            mode_real = pairs[pl.ds(t * channels + c, 1), pl.ds(0, wide)]
            mode_imag = pairs[pl.ds(t * channels + c, 1), pl.ds(wide, wide)]
            weight_real = mixers[pl.ds(c * channels, channels), :]
            weight_imag = mixers[pl.ds(square + c * channels, channels), :]
            real += mode_real * weight_real - mode_imag * weight_imag
            imag += mode_real * weight_imag + mode_imag * weight_real
        mixed[pl.ds(t * channels, channels), pl.ds(0, wide)] = real
        mixed[pl.ds(t * channels, channels), pl.ds(wide, wide)] = imag
    cells = dot(mixed[...].astype(BF16), x_back[...]).astype(BF16)
    for i in range(n_gx):
        going[i] = cells[:, i * LANES : (i + 1) * LANES]

    each(count, lambda s: second(s, me).start())
    back[me] = going[my_x]
    each(count, lambda s: second(s, source(s)).wait_recv())
    blocks = count // MZ
    for kz in range(MZ):
        for block in range(blocks):
            order[block, pl.ds(kz, fields, stride=MZ), :] = back[kz * blocks + block].astype(
                F32
            )[:fields]
    for block in range(blocks):
        out[:, pl.ds(block * LANES, LANES)] = order[block].astype(BF16)
    each(count, lambda s: first(s, me).wait_send())
    each(count, lambda s: second(s, me).wait_send())


def inverse_kernel(
    snapshots, channels, plume, cells, y_back, z_back, pointwise, bias, out, spectral
):
    x = pl.program_id(0)
    half = lax.axis_index("gy")
    fields, _, rows_y, depth = plume.shape
    group = z_back.shape[1] // depth
    table = y_back[half, x]
    grid_modes = dot_lanes(table, cells[...]).astype(BF16)
    real, imag = grid_modes[:rows_y], grid_modes[rows_y:]
    width = group * MZ
    for g in range(fields // group):
        both = jnp.concatenate(
            [real[:, g * width : (g + 1) * width], imag[:, g * width : (g + 1) * width]], axis=1
        )
        values = dot(both, z_back[...])
        for j in range(group):
            spectral[g * group + j] = values[:, j * depth : (j + 1) * depth]

    for t in range(snapshots):
        def strip(i, _, t=t):
            base = pl.multiple_of(i * 2 * TILE, 2 * TILE)
            fld = pl.ds(t * channels, channels)
            block = plume[fld, 0, pl.ds(base, 2 * TILE), :]
            pair = jnp.concatenate(
                [
                    block[:, :TILE].reshape(channels * TILE, depth),
                    block[:, TILE:].reshape(channels * TILE, depth),
                ],
                axis=1,
            )
            local = dot(pointwise[...], pair)
            for h in range(2):
                rows = pl.ds(base + h * TILE, TILE)
                value = local[:, h * depth : (h + 1) * depth].reshape(channels, TILE, depth)
                value = value + spectral[fld, rows, :] + bias[...]
                value = 0.5 * value * (1.0 + lax.erf(value * math.sqrt(0.5)))
                out[fld, 0, rows, :] = value.astype(BF16)
            return 0

        lax.fori_loop(0, rows_y // (2 * TILE), strip, 0)


def body(n_gx, n_gy, plume_state, spectral_weight, pointwise_weight, channel_bias):
    snapshots, channels, rows_x, rows_y, depth = plume_state.shape
    fields = snapshots * channels
    pair_rows = spectral_weight.shape[1]
    count = n_gx * n_gy
    blocks = MY // pair_rows
    group = LANES // MZ
    slot = up(fields, TILE)
    wide = up(pair_rows * MX, LANES)
    z_forward, y_forward, x_forward, x_back, y_back, z_back = tables(
        n_gx, n_gy, rows_x, rows_y, depth, pair_rows, group
    )
    whole = pl.BlockSpec(memory_space=pltpu.VMEM)
    limit = 50 * 2**20
    steps = fields // group
    sent = pl.pallas_call(
        functools.partial(forward_kernel, fields, steps),
        grid=(steps,),
        out_shape=jax.ShapeDtypeStruct((count, slot, LANES), BF16),
        in_specs=[
            pl.BlockSpec((group, rows_x * rows_y, depth), lambda g: (g, 0, 0)),
            whole,
            whole,
        ],
        out_specs=pl.BlockSpec((count, slot, LANES), lambda g: (0, 0, 0)),
        scratch_shapes=[pltpu.VMEM((blocks, slot * MZ, LANES), F32)],
        compiler_params=pltpu.CompilerParams(vmem_limit_bytes=limit),
        name="forward",
    )(plume_state.reshape(fields, rows_x * rows_y, depth), z_forward, y_forward)

    weights = spectral_weight.reshape(pair_rows * MX, -1)
    weights = jnp.pad(weights, [(0, wide - pair_rows * MX), (0, 0)])
    sems = pltpu.SemaphoreType.DMA((count,))
    cells = pl.pallas_call(
        functools.partial(modes_kernel, n_gx, n_gy, snapshots, channels),
        out_shape=jax.ShapeDtypeStruct((fields * MZ, blocks * LANES), BF16),
        in_specs=[whole] * 4,
        out_specs=whole,
        scratch_shapes=[
            pltpu.VMEM((count, slot, LANES), BF16),
            pltpu.VMEM((count, slot, LANES), BF16),
            pltpu.VMEM((n_gx, slot, LANES), BF16),
            pltpu.VMEM((up(weights.shape[1], LANES), wide), F32),
            pltpu.VMEM((slot, 2 * wide), F32),
            pltpu.VMEM((slot, 2 * wide), F32),
            pltpu.VMEM((blocks, fields * MZ, LANES), F32),
            sems, sems, sems, sems,
        ],
        compiler_params=pltpu.CompilerParams(
            vmem_limit_bytes=limit, collective_id=0, has_side_effects=True
        ),
        name="modes",
    )(sent, weights, x_forward, x_back)

    pointwise = (
        pointwise_weight.T[:, None, :, None] * jnp.eye(TILE, dtype=BF16)[None, :, None, :]
    ).reshape(channels * TILE, channels * TILE)
    bias = jnp.broadcast_to(channel_bias[:, None, None], (channels, 1, depth))
    state = plume_state.reshape(fields, rows_x, rows_y, depth)
    slab = pl.BlockSpec((fields, 1, rows_y, depth), lambda x: (0, x, 0, 0))
    result = pl.pallas_call(
        functools.partial(inverse_kernel, snapshots, channels),
        grid=(rows_x,),
        out_shape=jax.ShapeDtypeStruct(state.shape, BF16),
        in_specs=[slab] + [whole] * 5,
        out_specs=slab,
        scratch_shapes=[pltpu.VMEM((fields, rows_y, depth), F32)],
        compiler_params=pltpu.CompilerParams(vmem_limit_bytes=limit),
        name="inverse",
    )(state, cells, y_back, z_back, pointwise, bias)
    return result.reshape(plume_state.shape)


def solution(mesh):
    placed = (P("groups", None, "gx", "gy", None), P("gy", "gx", None, None), P(), P())
    return jax.shard_map(
        functools.partial(body, mesh.shape["gx"], mesh.shape["gy"]),
        mesh=mesh,
        in_specs=placed,
        out_specs=P("groups", None, "gx", "gy", None),
        check_vma=False,
    )
```

```python
import functools
import math

import jax
import jax.numpy as jnp
import ml_dtypes
import numpy as np
from jax import lax
from jax.experimental import pallas as pl
from jax.experimental.pallas import tpu as pltpu
from jax.sharding import PartitionSpec as P

MX = 24
MY = 16
MZ = 16
LANES = 128
TILE = 16
MESH = pl.DeviceIdType.MESH
F32 = jnp.float32
BF16 = jnp.bfloat16


def retained(kept, length):
    indices = np.arange(kept)
    return np.where(indices < kept // 2, indices, length - kept + indices)


def phases(freq_ids, positions, length):
    product = freq_ids[:, None] * positions[None, :] % length
    return np.float32(2.0 * math.pi / length) * product.astype(np.float32)


def forward_table(freq_ids, positions, length):
    angles = phases(freq_ids, positions, length).T
    cosine, sine = np.cos(angles), np.sin(angles)
    return np.stack([np.stack([cosine, -sine], 1), np.stack([sine, cosine], 1)], 1)


def inverse_table(freq_ids, positions, length):
    angles = phases(freq_ids, positions, length)
    cosine, sine = np.cos(angles), np.sin(angles)
    return np.stack([np.stack([cosine, sine], 1), np.stack([-sine, cosine], 1)], 0)


def up(value, step):
    return -(-value // step) * step


def pad_last(table, width):
    return np.pad(table, [(0, 0)] * (table.ndim - 1) + [(0, width - table.shape[-1])])


def tables(n_gx, n_gy, rows_x, rows_y, depth, pair_rows, group):
    length_x, length_y = n_gx * rows_x, n_gy * rows_y
    blocks = MY // pair_rows
    lanes_l = up(pair_rows * MX, LANES)
    angles = phases(np.arange(MZ), np.arange(depth), depth)
    z_forward = np.concatenate([np.cos(angles), -np.sin(angles)], 0)

    y_ids, x_ids = retained(MY, length_y), retained(MX, length_x)
    eye_x, eye_m = np.eye(rows_x), np.eye(pair_rows)
    fy = forward_table(y_ids, np.arange(length_y), length_y)
    fy = fy.reshape(n_gy, rows_y, 2, 2, blocks, pair_rows)
    y_forward = np.einsum("gypqbm,xw->gpxybwqm", fy, eye_x)
    y_forward = y_forward.reshape(n_gy, 2 * rows_x * rows_y, blocks, -1)
    y_forward = pad_last(y_forward, LANES).reshape(n_gy, 2 * rows_x * rows_y, blocks * LANES)

    fx = forward_table(x_ids, np.arange(length_x), length_x).reshape(n_gx, rows_x, 2, 2, MX)
    x_forward = np.einsum("ixqpk,mn->pnkixqm", fx, eye_m).reshape(2, pair_rows * MX, n_gx, -1)
    x_forward = pad_last(x_forward, LANES).reshape(2, pair_rows * MX, n_gx * LANES)
    x_forward = np.pad(x_forward, [(0, 0), (0, lanes_l - pair_rows * MX), (0, 0)])
    x_forward = x_forward.reshape(2 * lanes_l, n_gx * LANES).T

    ix = inverse_table(x_ids, np.arange(length_x), length_x).reshape(2, MX, 2, n_gx, rows_x)
    x_back = np.einsum("qkpix,mn->qnkixpm", ix, eye_m).reshape(2, pair_rows * MX, n_gx, -1)
    x_back = pad_last(x_back, LANES).reshape(2, pair_rows * MX, n_gx * LANES)
    x_back = np.pad(x_back, [(0, 0), (0, lanes_l - pair_rows * MX), (0, 0)])
    x_back = x_back.reshape(2 * lanes_l, n_gx * LANES)

    iy = inverse_table(y_ids, np.arange(length_y), length_y)
    iy = iy.reshape(2, blocks, pair_rows, 2, n_gy, rows_y)
    y_back = np.einsum("qbmpgy,xw->gpxybwqm", iy, eye_x)
    y_back = y_back.reshape(n_gy, 2, rows_x * rows_y, blocks, -1)
    y_back = pad_last(y_back, LANES).reshape(n_gy, 2, rows_x * rows_y, blocks * LANES)

    doubling = np.where(np.arange(MZ) == 0, 1.0, 2.0)[:, None]
    iz = np.stack([doubling * np.cos(angles), -doubling * np.sin(angles)], 0)
    iz = iz.astype(ml_dtypes.bfloat16).astype(np.float32) / (length_x * length_y * depth)
    z_back = np.einsum("pkz,jh->pjkhz", iz, np.eye(group))
    z_back = z_back.reshape(2 * group * MZ, group * depth)
    return [
        jnp.asarray(np.ascontiguousarray(t, dtype=np.float32).astype(ml_dtypes.bfloat16))
        for t in (z_forward, y_forward, x_forward, x_back, y_back, z_back)
    ]


def dot(a, b):
    return jnp.dot(a, b, preferred_element_type=F32)


def dot_lanes(a, b):
    return lax.dot_general(a, b, (((1,), (1,)), ((), ())), preferred_element_type=F32)


def each(count, one):
    if count <= 16:
        for s in range(1, count):
            one(s)
    else:
        lax.fori_loop(1, count, lambda s, _: (one(s), 0)[1], 0)


def modes_kernel(
    n_gx, n_gy, snapshots, channels, group,
    plume_in, z_forward, y_forward, weights_in, x_forward_in, x_back_in, pointwise, spread,
    out, local_out,
    plume, weights, x_forward, x_back, rows, sent,
    landed, back, going, mixers, pairs, mixed, order, local, kron,
    in_sem, table_sem, local_sem, send_one, recv_one, send_two, recv_two,
):
    count = n_gx * n_gy
    my_x, my_y = lax.axis_index("gx"), lax.axis_index("gy")
    me = my_y * n_gx + my_x
    fields = snapshots * channels
    wide = mixers.shape[1]
    blocks = count // MZ
    slot_rows = sent.shape[1]
    steps = fields // group

    def device(index):
        return {"gx": lax.rem(index, n_gx), "gy": lax.div(index, n_gx)}

    def chunk_in(g):
        part = pl.ds(g * group, group)
        return pltpu.make_async_copy(plume_in.at[part], plume.at[part], in_sem.at[g])

    for g in range(steps):
        chunk_in(g).start()
    held = [
        pltpu.make_async_copy(src, dst, table_sem.at[i])
        for i, (src, dst) in enumerate(
            [(weights_in, weights), (x_forward_in, x_forward), (x_back_in, x_back)]
        )
    ]
    for copy in held:
        copy.start()

    barrier = pltpu.get_barrier_semaphore()

    def greet(s):
        peer = lax.rem(me + s, count)
        pl.semaphore_signal(barrier, inc=1, device_id=device(peer), device_id_type=MESH)

    each(count, greet)
    size = channels * TILE
    scaled = dot_lanes(dot_lanes(spread[...], pointwise[...]).astype(BF16), spread[...])
    at_row = lax.broadcasted_iota(jnp.int32, (size, size), 0) % TILE
    at_column = lax.broadcasted_iota(jnp.int32, (size, size), 1) % TILE
    kron[...] = jnp.where(at_row == at_column, scaled, 0.0).astype(BF16)

    rows[:, pl.ds(fields * MZ, (slot_rows - fields) * MZ), :] = jnp.zeros(
        (blocks, (slot_rows - fields) * MZ, LANES), F32
    )
    for g in range(steps):
        chunk_in(g).wait()
        parts = []
        for j in range(group):
            modes = dot_lanes(z_forward[...], plume[g * group + j]).astype(BF16)
            parts.append(jnp.concatenate([modes[:MZ], modes[MZ:]], axis=1))
        terms = dot(jnp.concatenate(parts, axis=0), y_forward[my_y])
        for block in range(blocks):
            rows[block, pl.ds(g * group * MZ, group * MZ), :] = terms[
                :, block * LANES : (block + 1) * LANES
            ]
    for kz in range(MZ):
        for block in range(blocks):
            sent[kz * blocks + block] = rows[block, pl.ds(kz, slot_rows, stride=MZ), :].astype(
                BF16
            )
    pl.semaphore_wait(barrier, count - 1)

    depth = plume.shape[2]

    def pointwise_of(t):
        fld = pl.ds(t * channels, channels)

        def strip(i, _):
            base = pl.multiple_of(i * 2 * TILE, 2 * TILE)
            block = plume[fld, pl.ds(base, 2 * TILE), :]
            pair = jnp.concatenate(
                [
                    block[:, :TILE].reshape(size, depth),
                    block[:, TILE:].reshape(size, depth),
                ],
                axis=1,
            )
            value = dot(kron[...], pair)
            for h in range(2):
                local[fld, pl.ds(base + h * TILE, TILE), :] = value[
                    :, h * depth : (h + 1) * depth
                ].reshape(channels, TILE, depth)
            return 0

        lax.fori_loop(0, plume.shape[1] // (2 * TILE), strip, 0)
        local_copy(t).start()

    def local_copy(t):
        fld = pl.ds(t * channels, channels)
        return pltpu.make_async_copy(local.at[fld], local_out.at[fld], local_sem.at[t])

    def first(s, at):
        peer = lax.rem(me + s, count)
        return pltpu.make_async_remote_copy(
            src_ref=sent.at[peer], dst_ref=landed.at[at],
            send_sem=send_one.at[s], recv_sem=recv_one.at[s],
            device_id=device(peer), device_id_type=MESH,
        )

    def second(s, at):
        peer = lax.rem(me + s, count)
        return pltpu.make_async_remote_copy(
            src_ref=going.at[lax.rem(peer, n_gx)], dst_ref=back.at[at],
            send_sem=send_two.at[s], recv_sem=recv_two.at[s],
            device_id=device(peer), device_id_type=MESH,
        )

    def source(s):
        return lax.rem(me + count - s, count)

    each(count, lambda s: first(s, me).start())
    landed[me] = sent[me]

    for copy in held:
        copy.wait()
    length = weights.shape[1]
    for at in range(0, length, LANES):
        width = min(LANES, length - at)
        chunk = weights[:, pl.ds(at, width)].astype(F32)
        if width < LANES:
            chunk = jnp.concatenate([chunk, jnp.zeros((wide, LANES - width), F32)], axis=1)
        mixers[pl.ds(at, LANES), :] = chunk.T
    pointwise_of(0)

    each(count, lambda s: first(s, source(s)).wait_recv())
    summed = []
    for i in range(n_gx):
        total = landed[i].astype(F32)
        for g in range(1, n_gy):
            total += landed[g * n_gx + i].astype(F32)
        summed.append(total.astype(BF16))
    pairs[...] = dot(jnp.concatenate(summed, axis=1), x_forward[...]).astype(BF16).astype(F32)

    square = channels * channels
    mixed[...] = jnp.zeros_like(mixed)
    for t in range(snapshots):
        real = jnp.zeros((channels, wide), F32)
        imag = jnp.zeros((channels, wide), F32)
        for c in range(channels):
            mode_real = pairs[pl.ds(t * channels + c, 1), pl.ds(0, wide)]
            mode_imag = pairs[pl.ds(t * channels + c, 1), pl.ds(wide, wide)]
            weight_real = mixers[pl.ds(c * channels, channels), :]
            weight_imag = mixers[pl.ds(square + c * channels, channels), :]
            real += mode_real * weight_real - mode_imag * weight_imag
            imag += mode_real * weight_imag + mode_imag * weight_real
        mixed[pl.ds(t * channels, channels), pl.ds(0, wide)] = real
        mixed[pl.ds(t * channels, channels), pl.ds(wide, wide)] = imag
    cells = dot(mixed[...].astype(BF16), x_back[...]).astype(BF16)
    for i in range(n_gx):
        going[i] = cells[:, i * LANES : (i + 1) * LANES]

    each(count, lambda s: second(s, me).start())
    back[me] = going[my_x]
    for t in range(1, snapshots):
        pointwise_of(t)
    each(count, lambda s: second(s, source(s)).wait_recv())
    for kz in range(MZ):
        for block in range(blocks):
            order[block, pl.ds(kz, fields, stride=MZ), :] = back[kz * blocks + block].astype(
                F32
            )[:fields]
    for block in range(blocks):
        out[:, pl.ds(block * LANES, LANES)] = order[block].astype(BF16)
    each(count, lambda s: first(s, me).wait_send())
    each(count, lambda s: second(s, me).wait_send())
    for t in range(snapshots):
        local_copy(t).wait()


E = (
    0.797884268412902, 0.03633414910206053, -3.3026689185494805e-05, -5.527339041578515e-05,
    3.974071266817981e-06, -1.3378326030725087e-07, 1.8139279592266355e-09,
)


def gelu(x):
    square = jnp.minimum(x * x, 30.25)
    series = jnp.full_like(x, E[-1])
    for term in E[-2::-1]:
        series = series * square + term
    half = 0.5 * x
    return half + half * jnp.tanh(x * series)


def inverse_kernel(channels, local, cells, y_back, z_back, bias, out):
    g = pl.program_id(0)
    half = lax.axis_index("gy")
    group, _, depth = local.shape
    both = jnp.concatenate(
        [dot_lanes(y_back[half, p], cells[...]).astype(BF16) for p in range(2)], axis=1
    )
    for j in range(0, group, 2):
        values = dot(both, z_back[:, j * depth : (j + 2) * depth])
        for h in range(2):
            level = bias[lax.rem(g * group + j + h, channels)]
            value = values[:, h * depth : (h + 1) * depth] + local[j + h] + level
            out[j + h] = gelu(value).astype(BF16)


def body(n_gx, n_gy, plume_state, spectral_weight, pointwise_weight, channel_bias):
    snapshots, channels, rows_x, rows_y, depth = plume_state.shape
    fields = snapshots * channels
    cells_xy = rows_x * rows_y
    pair_rows = spectral_weight.shape[1]
    count = n_gx * n_gy
    blocks = MY // pair_rows
    group = LANES // MZ
    slot = up(fields, TILE)
    wide = up(pair_rows * MX, LANES)
    z_forward, y_forward, x_forward, x_back, y_back, z_back = tables(
        n_gx, n_gy, rows_x, rows_y, depth, pair_rows, group
    )
    spread = jnp.asarray(np.repeat(np.eye(channels), TILE, axis=0).astype(ml_dtypes.bfloat16))
    whole = pl.BlockSpec(memory_space=pltpu.VMEM)
    anywhere = pl.BlockSpec(memory_space=pl.ANY)
    limit = 60 * 2**20
    steps = fields // group
    weights = spectral_weight.reshape(pair_rows * MX, -1)
    weights = jnp.pad(weights, [(0, wide - pair_rows * MX), (0, 0)])
    state = plume_state.reshape(fields, cells_xy, depth)
    sems = pltpu.SemaphoreType.DMA((count,))
    cells, local = pl.pallas_call(
        functools.partial(modes_kernel, n_gx, n_gy, snapshots, channels, group),
        out_shape=(
            jax.ShapeDtypeStruct((fields * MZ, blocks * LANES), BF16),
            jax.ShapeDtypeStruct(state.shape, F32),
        ),
        in_specs=[anywhere, whole, whole, anywhere, anywhere, anywhere, whole, whole],
        out_specs=(whole, anywhere),
        scratch_shapes=[
            pltpu.VMEM(state.shape, BF16),
            pltpu.VMEM(weights.shape, BF16),
            pltpu.VMEM(x_forward.shape, BF16),
            pltpu.VMEM(x_back.shape, BF16),
            pltpu.VMEM((blocks, slot * MZ, LANES), F32),
            pltpu.VMEM((count, slot, LANES), BF16),
            pltpu.VMEM((count, slot, LANES), BF16),
            pltpu.VMEM((count, slot, LANES), BF16),
            pltpu.VMEM((n_gx, slot, LANES), BF16),
            pltpu.VMEM((up(weights.shape[1], LANES), wide), F32),
            pltpu.VMEM((slot, 2 * wide), F32),
            pltpu.VMEM((slot, 2 * wide), F32),
            pltpu.VMEM((blocks, fields * MZ, LANES), F32),
            pltpu.VMEM(state.shape, F32),
            pltpu.VMEM((channels * TILE, channels * TILE), BF16),
            pltpu.SemaphoreType.DMA((steps,)),
            pltpu.SemaphoreType.DMA((3,)),
            pltpu.SemaphoreType.DMA((snapshots,)),
            sems, sems, sems, sems,
        ],
        compiler_params=pltpu.CompilerParams(
            vmem_limit_bytes=limit, collective_id=0, has_side_effects=True
        ),
        name="modes",
    )(state, z_forward, y_forward, weights, x_forward, x_back, pointwise_weight, spread)

    slab = pl.BlockSpec((group, cells_xy, depth), lambda g: (g, 0, 0))
    result = pl.pallas_call(
        functools.partial(inverse_kernel, channels),
        grid=(steps,),
        out_shape=jax.ShapeDtypeStruct(state.shape, BF16),
        in_specs=[
            slab,
            pl.BlockSpec((group * MZ, blocks * LANES), lambda g: (g, 0)),
            whole,
            whole,
            pl.BlockSpec(memory_space=pltpu.SMEM),
        ],
        out_specs=slab,
        compiler_params=pltpu.CompilerParams(vmem_limit_bytes=limit),
        name="inverse",
    )(local, cells, y_back, z_back, channel_bias)
    return result.reshape(plume_state.shape)


def solution(mesh):
    placed = (P("groups", None, "gx", "gy", None), P("gy", "gx", None, None), P(), P())
    return jax.shard_map(
        functools.partial(body, mesh.shape["gx"], mesh.shape["gy"]),
        mesh=mesh,
        in_specs=placed,
        out_specs=P("groups", None, "gx", "gy", None),
        check_vma=False,
    )
```

```python
import functools
import math

import jax
import jax.numpy as jnp
import ml_dtypes
import numpy as np
from jax import lax
from jax.experimental import pallas as pl
from jax.experimental.pallas import tpu as pltpu
from jax.sharding import PartitionSpec as P

MX = 24
MY = 16
MZ = 16
LANES = 128
TILE = 16
HALF = 8
MESH = pl.DeviceIdType.MESH
F32 = jnp.float32
BF16 = jnp.bfloat16


def retained(kept, length):
    indices = np.arange(kept)
    return np.where(indices < kept // 2, indices, length - kept + indices)


def phases(freq_ids, positions, length):
    product = freq_ids[:, None] * positions[None, :] % length
    return np.float32(2.0 * math.pi / length) * product.astype(np.float32)


def forward_table(freq_ids, positions, length):
    angles = phases(freq_ids, positions, length).T
    cosine, sine = np.cos(angles), np.sin(angles)
    return np.stack([np.stack([cosine, -sine], 1), np.stack([sine, cosine], 1)], 1)


def inverse_table(freq_ids, positions, length):
    angles = phases(freq_ids, positions, length)
    cosine, sine = np.cos(angles), np.sin(angles)
    return np.stack([np.stack([cosine, sine], 1), np.stack([-sine, cosine], 1)], 0)


def up(value, step):
    return -(-value // step) * step


def pad_last(table, width):
    return np.pad(table, [(0, 0)] * (table.ndim - 1) + [(0, width - table.shape[-1])])


def tables(n_gx, n_gy, rows_x, rows_y, depth, pair_rows, group):
    length_x, length_y = n_gx * rows_x, n_gy * rows_y
    blocks = MY // pair_rows
    lanes_l = up(pair_rows * MX, LANES)
    angles = phases(np.arange(MZ), np.arange(depth), depth)
    z_forward = np.concatenate([np.cos(angles), -np.sin(angles)], 0)

    y_ids, x_ids = retained(MY, length_y), retained(MX, length_x)
    eye_x, eye_m = np.eye(rows_x), np.eye(pair_rows)
    fy = forward_table(y_ids, np.arange(length_y), length_y)
    fy = fy.reshape(n_gy, rows_y, 2, 2, blocks, pair_rows)
    y_forward = np.einsum("gypqbm,xw->gpxybwqm", fy, eye_x)
    y_forward = y_forward.reshape(n_gy, 2 * rows_x * rows_y, blocks, -1)
    y_forward = pad_last(y_forward, LANES).reshape(n_gy, 2 * rows_x * rows_y, blocks * LANES)

    fx = forward_table(x_ids, np.arange(length_x), length_x).reshape(n_gx, rows_x, 2, 2, MX)
    x_forward = np.einsum("ixqpk,mn->pnkixqm", fx, eye_m).reshape(2, pair_rows * MX, n_gx, -1)
    x_forward = pad_last(x_forward, LANES).reshape(2, pair_rows * MX, n_gx * LANES)
    x_forward = np.pad(x_forward, [(0, 0), (0, lanes_l - pair_rows * MX), (0, 0)])
    x_forward = x_forward.reshape(2 * lanes_l, n_gx * LANES).T

    ix = inverse_table(x_ids, np.arange(length_x), length_x).reshape(2, MX, 2, n_gx, rows_x)
    x_back = np.einsum("qkpix,mn->qnkixpm", ix, eye_m).reshape(2, pair_rows * MX, n_gx, -1)
    x_back = pad_last(x_back, LANES).reshape(2, pair_rows * MX, n_gx * LANES)
    x_back = np.pad(x_back, [(0, 0), (0, lanes_l - pair_rows * MX), (0, 0)])
    x_back = x_back.reshape(2 * lanes_l, n_gx * LANES)

    iy = inverse_table(y_ids, np.arange(length_y), length_y)
    iy = iy.reshape(2, blocks, pair_rows, 2, n_gy, rows_y)
    y_back = np.einsum("qbmpgy,xw->gpxybwqm", iy, eye_x)
    y_back = y_back.reshape(n_gy, 2, rows_x * rows_y, blocks, -1)
    y_back = pad_last(y_back, LANES).reshape(n_gy, 2, rows_x * rows_y, blocks * LANES)

    doubling = np.where(np.arange(MZ) == 0, 1.0, 2.0)[:, None]
    iz = np.stack([doubling * np.cos(angles), -doubling * np.sin(angles)], 0)
    iz = iz.astype(ml_dtypes.bfloat16).astype(np.float32) / (length_x * length_y * depth)
    z_back = np.einsum("pkz,jh->pjkhz", iz, np.eye(group))
    z_back = z_back.reshape(2 * group * MZ, group * depth)
    return [
        jnp.asarray(np.ascontiguousarray(t, dtype=np.float32).astype(ml_dtypes.bfloat16))
        for t in (z_forward, y_forward, x_forward, x_back, y_back, z_back)
    ]


def dot(a, b):
    return jnp.dot(a, b, preferred_element_type=F32)


def dot_lanes(a, b):
    return lax.dot_general(a, b, (((1,), (1,)), ((), ())), preferred_element_type=F32)


def each(count, one):
    if count <= 16:
        for s in range(1, count):
            one(s)
    else:
        lax.fori_loop(1, count, lambda s, _: (one(s), 0)[1], 0)


def modes_kernel(
    n_gx, n_gy, snapshots, channels, group,
    plume_in, z_forward, y_forward, weights_in, x_forward_in, x_back_in, pointwise, spread,
    out, local_out,
    plume, weights, x_forward, x_back, rows, sent,
    landed, back, going, mixers, pairs, mixed, order, local, kron,
    in_sem, table_sem, local_sem, send_one, recv_one, send_two, recv_two,
):
    count = n_gx * n_gy
    my_x, my_y = lax.axis_index("gx"), lax.axis_index("gy")
    me = my_y * n_gx + my_x
    fields = snapshots * channels
    wide = mixers.shape[1]
    blocks = count // MZ
    slot_rows = sent.shape[1]
    steps = fields // group

    def device(index):
        return {"gx": lax.rem(index, n_gx), "gy": lax.div(index, n_gx)}

    def chunk_in(g):
        part = pl.ds(g * group, group)
        return pltpu.make_async_copy(plume_in.at[part], plume.at[part], in_sem.at[g])

    for g in range(steps):
        chunk_in(g).start()
    held = [
        pltpu.make_async_copy(src, dst, table_sem.at[i])
        for i, (src, dst) in enumerate(
            [(weights_in, weights), (x_forward_in, x_forward), (x_back_in, x_back)]
        )
    ]
    for copy in held:
        copy.start()

    barrier = pltpu.get_barrier_semaphore()

    def greet(s):
        peer = lax.rem(me + s, count)
        pl.semaphore_signal(barrier, inc=1, device_id=device(peer), device_id_type=MESH)

    each(count, greet)
    size = channels * HALF
    scaled = dot_lanes(dot_lanes(spread[...], pointwise[...]).astype(BF16), spread[...])
    at_row = lax.broadcasted_iota(jnp.int32, (size, size), 0) % HALF
    at_column = lax.broadcasted_iota(jnp.int32, (size, size), 1) % HALF
    kron[...] = jnp.where(at_row == at_column, scaled, 0.0).astype(BF16)

    rows[:, pl.ds(fields * MZ, (slot_rows - fields) * MZ), :] = jnp.zeros(
        (blocks, (slot_rows - fields) * MZ, LANES), F32
    )
    for g in range(steps):
        chunk_in(g).wait()
        parts = []
        for j in range(group):
            modes = dot_lanes(z_forward[...], plume[g * group + j]).astype(BF16)
            parts.append(jnp.concatenate([modes[:MZ], modes[MZ:]], axis=1))
        terms = dot(jnp.concatenate(parts, axis=0), y_forward[my_y])
        for block in range(blocks):
            rows[block, pl.ds(g * group * MZ, group * MZ), :] = terms[
                :, block * LANES : (block + 1) * LANES
            ]
    for kz in range(MZ):
        for block in range(blocks):
            sent[kz * blocks + block] = rows[block, pl.ds(kz, slot_rows, stride=MZ), :].astype(
                BF16
            )
    pl.semaphore_wait(barrier, count - 1)

    depth = plume.shape[2]

    def pointwise_of(t):
        fld = pl.ds(t * channels, channels)

        def strip(i, _):
            base = pl.ds(pl.multiple_of(i * TILE, TILE), TILE)
            block = plume[fld, base, :].astype(F32)
            pair = jnp.concatenate(
                [block[:, h : h + HALF].reshape(size, depth) for h in (0, HALF)], axis=1
            )
            value = dot(kron[...], pair.astype(BF16))
            local[fld, base, :] = jnp.concatenate(
                [
                    value[:, h : h + depth].reshape(channels, HALF, depth)
                    for h in (0, depth)
                ],
                axis=1,
            ).astype(BF16)
            return 0

        lax.fori_loop(0, plume.shape[1] // TILE, strip, 0, unroll=8)
        local_copy(t).start()

    def local_copy(t):
        fld = pl.ds(t * channels, channels)
        return pltpu.make_async_copy(local.at[fld], local_out.at[fld], local_sem.at[t])

    def first(s, at):
        peer = lax.rem(me + s, count)
        return pltpu.make_async_remote_copy(
            src_ref=sent.at[peer], dst_ref=landed.at[at],
            send_sem=send_one.at[s], recv_sem=recv_one.at[s],
            device_id=device(peer), device_id_type=MESH,
        )

    def second(s, at):
        peer = lax.rem(me + s, count)
        return pltpu.make_async_remote_copy(
            src_ref=going.at[lax.rem(peer, n_gx)], dst_ref=back.at[at],
            send_sem=send_two.at[s], recv_sem=recv_two.at[s],
            device_id=device(peer), device_id_type=MESH,
        )

    def source(s):
        return lax.rem(me + count - s, count)

    each(count, lambda s: first(s, me).start())
    landed[me] = sent[me]

    for copy in held:
        copy.wait()
    length = weights.shape[1]
    for at in range(0, length, LANES):
        width = min(LANES, length - at)
        chunk = weights[:, pl.ds(at, width)].astype(F32)
        if width < LANES:
            chunk = jnp.concatenate([chunk, jnp.zeros((wide, LANES - width), F32)], axis=1)
        mixers[pl.ds(at, LANES), :] = chunk.T
    pointwise_of(0)

    each(count, lambda s: first(s, source(s)).wait_recv())
    summed = []
    for i in range(n_gx):
        total = landed[i].astype(F32)
        for g in range(1, n_gy):
            total += landed[g * n_gx + i].astype(F32)
        summed.append(total.astype(BF16))
    pairs[...] = dot(jnp.concatenate(summed, axis=1), x_forward[...]).astype(BF16).astype(F32)

    square = channels * channels
    mixed[...] = jnp.zeros_like(mixed)
    for t in range(snapshots):
        real = jnp.zeros((channels, wide), F32)
        imag = jnp.zeros((channels, wide), F32)
        for c in range(channels):
            mode_real = pairs[pl.ds(t * channels + c, 1), pl.ds(0, wide)]
            mode_imag = pairs[pl.ds(t * channels + c, 1), pl.ds(wide, wide)]
            weight_real = mixers[pl.ds(c * channels, channels), :]
            weight_imag = mixers[pl.ds(square + c * channels, channels), :]
            real += mode_real * weight_real - mode_imag * weight_imag
            imag += mode_real * weight_imag + mode_imag * weight_real
        mixed[pl.ds(t * channels, channels), pl.ds(0, wide)] = real
        mixed[pl.ds(t * channels, channels), pl.ds(wide, wide)] = imag
    cells = dot(mixed[...].astype(BF16), x_back[...]).astype(BF16)
    for i in range(n_gx):
        going[i] = cells[:, i * LANES : (i + 1) * LANES]

    each(count, lambda s: second(s, me).start())
    back[me] = going[my_x]
    for t in range(1, snapshots):
        pointwise_of(t)
    each(count, lambda s: second(s, source(s)).wait_recv())
    for kz in range(MZ):
        for block in range(blocks):
            order[block, pl.ds(kz, fields, stride=MZ), :] = back[kz * blocks + block].astype(
                F32
            )[:fields]
    for block in range(blocks):
        out[:, pl.ds(block * LANES, LANES)] = order[block].astype(BF16)
    each(count, lambda s: first(s, me).wait_send())
    each(count, lambda s: second(s, me).wait_send())
    for t in range(snapshots):
        local_copy(t).wait()


def gelu(x):
    half = 0.5 * x
    return half + half * lax.erf(x * math.sqrt(0.5))


def inverse_kernel(channels, local, cells, y_back, z_back, bias, out):
    g = pl.program_id(0)
    half = lax.axis_index("gy")
    group, _, depth = local.shape
    both = jnp.concatenate(
        [dot_lanes(y_back[half, p], cells[...]).astype(BF16) for p in range(2)], axis=1
    )
    for j in range(0, group, 2):
        values = dot(both, z_back[:, j * depth : (j + 2) * depth])
        for h in range(2):
            level = bias[lax.rem(g * group + j + h, channels)]
            value = values[:, h * depth : (h + 1) * depth] + local[j + h].astype(F32) + level
            out[j + h] = gelu(value).astype(BF16)


def body(n_gx, n_gy, plume_state, spectral_weight, pointwise_weight, channel_bias):
    snapshots, channels, rows_x, rows_y, depth = plume_state.shape
    fields = snapshots * channels
    cells_xy = rows_x * rows_y
    pair_rows = spectral_weight.shape[1]
    count = n_gx * n_gy
    blocks = MY // pair_rows
    group = LANES // MZ
    slot = up(fields, TILE)
    wide = up(pair_rows * MX, LANES)
    z_forward, y_forward, x_forward, x_back, y_back, z_back = tables(
        n_gx, n_gy, rows_x, rows_y, depth, pair_rows, group
    )
    spread = jnp.asarray(np.repeat(np.eye(channels), HALF, axis=0).astype(ml_dtypes.bfloat16))
    whole = pl.BlockSpec(memory_space=pltpu.VMEM)
    anywhere = pl.BlockSpec(memory_space=pl.ANY)
    limit = 60 * 2**20
    steps = fields // group
    weights = spectral_weight.reshape(pair_rows * MX, -1)
    weights = jnp.pad(weights, [(0, wide - pair_rows * MX), (0, 0)])
    state = plume_state.reshape(fields, cells_xy, depth)
    sems = pltpu.SemaphoreType.DMA((count,))
    cells, local = pl.pallas_call(
        functools.partial(modes_kernel, n_gx, n_gy, snapshots, channels, group),
        out_shape=(
            jax.ShapeDtypeStruct((fields * MZ, blocks * LANES), BF16),
            jax.ShapeDtypeStruct(state.shape, BF16),
        ),
        in_specs=[anywhere, whole, whole, anywhere, anywhere, anywhere, whole, whole],
        out_specs=(whole, anywhere),
        scratch_shapes=[
            pltpu.VMEM(state.shape, BF16),
            pltpu.VMEM(weights.shape, BF16),
            pltpu.VMEM(x_forward.shape, BF16),
            pltpu.VMEM(x_back.shape, BF16),
            pltpu.VMEM((blocks, slot * MZ, LANES), F32),
            pltpu.VMEM((count, slot, LANES), BF16),
            pltpu.VMEM((count, slot, LANES), BF16),
            pltpu.VMEM((count, slot, LANES), BF16),
            pltpu.VMEM((n_gx, slot, LANES), BF16),
            pltpu.VMEM((up(weights.shape[1], LANES), wide), F32),
            pltpu.VMEM((slot, 2 * wide), F32),
            pltpu.VMEM((slot, 2 * wide), F32),
            pltpu.VMEM((blocks, fields * MZ, LANES), F32),
            pltpu.VMEM(state.shape, BF16),
            pltpu.VMEM((channels * HALF, channels * HALF), BF16),
            pltpu.SemaphoreType.DMA((steps,)),
            pltpu.SemaphoreType.DMA((3,)),
            pltpu.SemaphoreType.DMA((snapshots,)),
            sems, sems, sems, sems,
        ],
        compiler_params=pltpu.CompilerParams(
            vmem_limit_bytes=limit, collective_id=0, has_side_effects=True
        ),
        name="modes",
    )(state, z_forward, y_forward, weights, x_forward, x_back, pointwise_weight, spread)

    slab = pl.BlockSpec((group, cells_xy, depth), lambda g: (g, 0, 0))
    result = pl.pallas_call(
        functools.partial(inverse_kernel, channels),
        grid=(steps,),
        out_shape=jax.ShapeDtypeStruct(state.shape, BF16),
        in_specs=[
            slab,
            pl.BlockSpec((group * MZ, blocks * LANES), lambda g: (g, 0)),
            whole,
            whole,
            pl.BlockSpec(memory_space=pltpu.SMEM),
        ],
        out_specs=slab,
        compiler_params=pltpu.CompilerParams(vmem_limit_bytes=limit),
        name="inverse",
    )(local, cells, y_back, z_back, channel_bias)
    return result.reshape(plume_state.shape)


def solution(mesh):
    placed = (P("groups", None, "gx", "gy", None), P("gy", "gx", None, None), P(), P())
    return jax.shard_map(
        functools.partial(body, mesh.shape["gx"], mesh.shape["gy"]),
        mesh=mesh,
        in_specs=placed,
        out_specs=P("groups", None, "gx", "gy", None),
        check_vma=False,
    )
```

```python
import functools
import math

import jax
import jax.numpy as jnp
import ml_dtypes
import numpy as np
from jax import lax
from jax.experimental import pallas as pl
from jax.experimental.pallas import tpu as pltpu
from jax.sharding import PartitionSpec as P

MX = 24
MY = 16
MZ = 16
LANES = 128
TILE = 16
HALF = 8
MESH = pl.DeviceIdType.MESH
F32 = jnp.float32
BF16 = jnp.bfloat16


def retained(kept, length):
    indices = np.arange(kept)
    return np.where(indices < kept // 2, indices, length - kept + indices)


def phases(freq_ids, positions, length):
    product = freq_ids[:, None] * positions[None, :] % length
    return np.float32(2.0 * math.pi / length) * product.astype(np.float32)


def forward_table(freq_ids, positions, length):
    angles = phases(freq_ids, positions, length).T
    cosine, sine = np.cos(angles), np.sin(angles)
    return np.stack([np.stack([cosine, -sine], 1), np.stack([sine, cosine], 1)], 1)


def inverse_table(freq_ids, positions, length):
    angles = phases(freq_ids, positions, length)
    cosine, sine = np.cos(angles), np.sin(angles)
    return np.stack([np.stack([cosine, sine], 1), np.stack([-sine, cosine], 1)], 0)


def up(value, step):
    return -(-value // step) * step


def pad_last(table, width):
    return np.pad(table, [(0, 0)] * (table.ndim - 1) + [(0, width - table.shape[-1])])


def tables(n_gx, n_gy, rows_x, rows_y, depth, pair_rows, group):
    length_x, length_y = n_gx * rows_x, n_gy * rows_y
    blocks = MY // pair_rows
    lanes_l = up(pair_rows * MX, LANES)
    angles = phases(np.arange(MZ), np.arange(depth), depth)
    z_forward = np.concatenate([np.cos(angles), -np.sin(angles)], 0)

    y_ids, x_ids = retained(MY, length_y), retained(MX, length_x)
    eye_x, eye_m = np.eye(rows_x), np.eye(pair_rows)
    fy = forward_table(y_ids, np.arange(length_y), length_y)
    fy = fy.reshape(n_gy, rows_y, 2, 2, blocks, pair_rows)
    y_forward = np.einsum("gypqbm,xw->gpxybwqm", fy, eye_x)
    y_forward = y_forward.reshape(n_gy, 2 * rows_x * rows_y, blocks, -1)
    y_forward = pad_last(y_forward, LANES).reshape(n_gy, 2 * rows_x * rows_y, blocks * LANES)

    fx = forward_table(x_ids, np.arange(length_x), length_x).reshape(n_gx, rows_x, 2, 2, MX)
    x_forward = np.einsum("ixqpk,mn->pnkixqm", fx, eye_m).reshape(2, pair_rows * MX, n_gx, -1)
    x_forward = pad_last(x_forward, LANES).reshape(2, pair_rows * MX, n_gx * LANES)
    x_forward = np.pad(x_forward, [(0, 0), (0, lanes_l - pair_rows * MX), (0, 0)])
    x_forward = x_forward.reshape(2 * lanes_l, n_gx * LANES).T

    ix = inverse_table(x_ids, np.arange(length_x), length_x).reshape(2, MX, 2, n_gx, rows_x)
    x_back = np.einsum("qkpix,mn->qnkixpm", ix, eye_m).reshape(2, pair_rows * MX, n_gx, -1)
    x_back = pad_last(x_back, LANES).reshape(2, pair_rows * MX, n_gx * LANES)
    x_back = np.pad(x_back, [(0, 0), (0, lanes_l - pair_rows * MX), (0, 0)])
    x_back = x_back.reshape(2 * lanes_l, n_gx * LANES)

    iy = inverse_table(y_ids, np.arange(length_y), length_y)
    iy = iy.reshape(2, blocks, pair_rows, 2, n_gy, rows_y)
    y_back = np.einsum("qbmpgy,xw->gpxybwqm", iy, eye_x)
    y_back = y_back.reshape(n_gy, 2, rows_x * rows_y, blocks, -1)
    y_back = pad_last(y_back, LANES).reshape(n_gy, 2, rows_x * rows_y, blocks * LANES)

    doubling = np.where(np.arange(MZ) == 0, 1.0, 2.0)[:, None]
    iz = np.stack([doubling * np.cos(angles), -doubling * np.sin(angles)], 0)
    iz = iz.astype(ml_dtypes.bfloat16).astype(np.float32) / (length_x * length_y * depth)
    z_back = np.einsum("pkz,jh->pjkhz", iz, np.eye(group))
    z_back = z_back.reshape(2 * group * MZ, group * depth)
    return [
        jnp.asarray(np.ascontiguousarray(t, dtype=np.float32).astype(ml_dtypes.bfloat16))
        for t in (z_forward, y_forward, x_forward, x_back, y_back, z_back)
    ]


def dot(a, b):
    return jnp.dot(a, b, preferred_element_type=F32)


def dot_lanes(a, b):
    return lax.dot_general(a, b, (((1,), (1,)), ((), ())), preferred_element_type=F32)


def each(count, one):
    if count <= 16:
        for s in range(1, count):
            one(s)
    else:
        lax.fori_loop(1, count, lambda s, _: (one(s), 0)[1], 0)


def modes_kernel(
    n_gx, n_gy, snapshots, channels, group,
    plume_in, z_forward, y_forward, weights_in, x_forward_in, x_back_in, pointwise, spread,
    out, local_out,
    plume, weights, x_forward, x_back, rows, sent,
    landed, back, going, mixers, pairs, mixed, order, local, kron,
    in_sem, table_sem, local_sem, send_one, recv_one, send_two, recv_two, send_on, recv_on,
):
    count = n_gx * n_gy
    my_x, my_y = lax.axis_index("gx"), lax.axis_index("gy")
    me = my_y * n_gx + my_x
    fields = snapshots * channels
    wide = mixers.shape[1]
    blocks = count // MZ
    slot_rows = sent.shape[1]
    steps = fields // group
    parts_out = slot_rows // TILE

    def device(index):
        return {"gx": lax.rem(index, n_gx), "gy": lax.div(index, n_gx)}

    def chunk_in(g):
        part = pl.ds(g * group, group)
        return pltpu.make_async_copy(plume_in.at[part], plume.at[part], in_sem.at[g])

    for g in range(steps):
        chunk_in(g).start()
    held = [
        pltpu.make_async_copy(src, dst, table_sem.at[i])
        for i, (src, dst) in enumerate(
            [(weights_in, weights), (x_forward_in, x_forward), (x_back_in, x_back)]
        )
    ]
    for copy in held:
        copy.start()

    barrier = pltpu.get_barrier_semaphore()

    def greet(s):
        peer = lax.rem(me + s, count)
        pl.semaphore_signal(barrier, inc=1, device_id=device(peer), device_id_type=MESH)

    each(count, greet)
    size = channels * HALF
    scaled = dot_lanes(dot_lanes(spread[...], pointwise[...]).astype(BF16), spread[...])
    at_row = lax.broadcasted_iota(jnp.int32, (size, size), 0) % HALF
    at_column = lax.broadcasted_iota(jnp.int32, (size, size), 1) % HALF
    kron[...] = jnp.where(at_row == at_column, scaled, 0.0).astype(BF16)

    def first(s, at, part):
        peer = lax.rem(me + s, count)
        band = pl.ds(part * TILE, TILE)
        return pltpu.make_async_remote_copy(
            src_ref=sent.at[peer, band], dst_ref=landed.at[at, band],
            send_sem=send_one.at[part, s], recv_sem=recv_one.at[part, s],
            device_id=device(peer), device_id_type=MESH,
        )

    def send_part(part):
        band = pl.ds(part * TILE, TILE)
        for kz in range(MZ):
            for block in range(blocks):
                taken = rows[block, pl.ds(part * TILE * MZ + kz, TILE, stride=MZ), :]
                sent[kz * blocks + block, band, :] = taken.astype(BF16)
        if part == 0:
            pl.semaphore_wait(barrier, count - 1)
        each(count, lambda s: first(s, me, part).start())

    def second(s, at):
        peer = lax.rem(my_x + s, n_gx)
        return pltpu.make_async_remote_copy(
            src_ref=going.at[peer], dst_ref=back.at[at],
            send_sem=send_two.at[s], recv_sem=recv_two.at[s],
            device_id={"gx": peer}, device_id_type=MESH,
        )

    def onward(h, s, owner_y):
        at = owner_y * n_gx + lax.rem(my_x + n_gx - s, n_gx)
        return pltpu.make_async_remote_copy(
            src_ref=back.at[at], dst_ref=back.at[at],
            send_sem=send_on.at[h, s], recv_sem=recv_on.at[h, s],
            device_id={"gy": lax.rem(my_y + h, n_gy)}, device_id_type=MESH,
        )

    def arrived(s):
        second(s, my_y * n_gx + lax.rem(my_x + n_gx - s, n_gx)).wait_recv()
        for h in range(1, n_gy):
            onward(h, s, my_y).start()

    def source(s):
        return lax.rem(me + count - s, count)

    rows[:, pl.ds(fields * MZ, (slot_rows - fields) * MZ), :] = jnp.zeros(
        (blocks, (slot_rows - fields) * MZ, LANES), F32
    )
    for g in range(steps):
        chunk_in(g).wait()
        parts = []
        for j in range(group):
            modes = dot_lanes(z_forward[...], plume[g * group + j]).astype(BF16)
            parts.append(jnp.concatenate([modes[:MZ], modes[MZ:]], axis=1))
        terms = dot(jnp.concatenate(parts, axis=0), y_forward[my_y])
        for block in range(blocks):
            rows[block, pl.ds(g * group * MZ, group * MZ), :] = terms[
                :, block * LANES : (block + 1) * LANES
            ]
        for part in range(parts_out):
            ready = min(-(-(part + 1) * TILE // group), steps) - 1
            if ready == g:
                send_part(part)

    depth = plume.shape[2]

    def pointwise_of(t):
        fld = pl.ds(t * channels, channels)

        def strip(i, _):
            base = pl.ds(pl.multiple_of(i * TILE, TILE), TILE)
            block = plume[fld, base, :].astype(F32)
            pair = jnp.concatenate(
                [block[:, h : h + HALF].reshape(size, depth) for h in (0, HALF)], axis=1
            )
            value = dot(kron[...], pair.astype(BF16))
            local[fld, base, :] = jnp.concatenate(
                [
                    value[:, h : h + depth].reshape(channels, HALF, depth)
                    for h in (0, depth)
                ],
                axis=1,
            ).astype(BF16)
            return 0

        lax.fori_loop(0, plume.shape[1] // TILE, strip, 0, unroll=8)
        local_copy(t).start()

    def local_copy(t):
        fld = pl.ds(t * channels, channels)
        return pltpu.make_async_copy(local.at[fld], local_out.at[fld], local_sem.at[t])

    landed[me] = sent[me]

    for copy in held:
        copy.wait()
    length = weights.shape[1]
    for at in range(0, length, LANES):
        width = min(LANES, length - at)
        chunk = weights[:, pl.ds(at, width)].astype(F32)
        if width < LANES:
            chunk = jnp.concatenate([chunk, jnp.zeros((wide, LANES - width), F32)], axis=1)
        mixers[pl.ds(at, LANES), :] = chunk.T
    pointwise_of(0)

    for part in range(parts_out):
        each(count, lambda s, part=part: first(s, source(s), part).wait_recv())
    summed = []
    for i in range(n_gx):
        total = landed[i].astype(F32)
        for g in range(1, n_gy):
            total += landed[g * n_gx + i].astype(F32)
        summed.append(total.astype(BF16))
    pairs[...] = dot(jnp.concatenate(summed, axis=1), x_forward[...]).astype(BF16).astype(F32)

    square = channels * channels
    mixed[...] = jnp.zeros_like(mixed)
    for t in range(snapshots):
        real = jnp.zeros((channels, wide), F32)
        imag = jnp.zeros((channels, wide), F32)
        for c in range(channels):
            mode_real = pairs[pl.ds(t * channels + c, 1), pl.ds(0, wide)]
            mode_imag = pairs[pl.ds(t * channels + c, 1), pl.ds(wide, wide)]
            weight_real = mixers[pl.ds(c * channels, channels), :]
            weight_imag = mixers[pl.ds(square + c * channels, channels), :]
            real += mode_real * weight_real - mode_imag * weight_imag
            imag += mode_real * weight_imag + mode_imag * weight_real
        mixed[pl.ds(t * channels, channels), pl.ds(0, wide)] = real
        mixed[pl.ds(t * channels, channels), pl.ds(wide, wide)] = imag
    cells = dot(mixed[...].astype(BF16), x_back[...]).astype(BF16)
    for i in range(n_gx):
        going[i] = cells[:, i * LANES : (i + 1) * LANES]

    each(n_gx, lambda s: second(s, me).start())
    back[me] = going[my_x]
    for h in range(1, n_gy):
        onward(h, 0, my_y).start()
    for t in range(1, snapshots):
        pointwise_of(t)
    each(n_gx, arrived)
    for h in range(1, n_gy):
        owner_y = lax.rem(my_y + n_gy - h, n_gy)
        onward(h, 0, owner_y).wait_recv()
        each(n_gx, lambda s, h=h, owner_y=owner_y: onward(h, s, owner_y).wait_recv())
    for kz in range(MZ):
        for block in range(blocks):
            order[block, pl.ds(kz, fields, stride=MZ), :] = back[kz * blocks + block].astype(
                F32
            )[:fields]
    for block in range(blocks):
        out[:, pl.ds(block * LANES, LANES)] = order[block].astype(BF16)
    for part in range(parts_out):
        each(count, lambda s, part=part: first(s, me, part).wait_send())
    each(n_gx, lambda s: second(s, me).wait_send())
    for h in range(1, n_gy):
        onward(h, 0, my_y).wait_send()
        each(n_gx, lambda s, h=h: onward(h, s, my_y).wait_send())
    for t in range(snapshots):
        local_copy(t).wait()


def gelu(x):
    half = 0.5 * x
    return half + half * lax.erf(x * math.sqrt(0.5))


def inverse_kernel(channels, local, cells, y_back, z_back, bias, out):
    g = pl.program_id(0)
    half = lax.axis_index("gy")
    group, _, depth = local.shape
    both = jnp.concatenate(
        [dot_lanes(y_back[half, p], cells[...]).astype(BF16) for p in range(2)], axis=1
    )
    for j in range(0, group, 2):
        values = dot(both, z_back[:, j * depth : (j + 2) * depth])
        for h in range(2):
            level = bias[lax.rem(g * group + j + h, channels)]
            value = values[:, h * depth : (h + 1) * depth] + local[j + h].astype(F32) + level
            out[j + h] = gelu(value).astype(BF16)


def body(n_gx, n_gy, plume_state, spectral_weight, pointwise_weight, channel_bias):
    snapshots, channels, rows_x, rows_y, depth = plume_state.shape
    fields = snapshots * channels
    cells_xy = rows_x * rows_y
    pair_rows = spectral_weight.shape[1]
    count = n_gx * n_gy
    blocks = MY // pair_rows
    group = LANES // MZ
    slot = up(fields, TILE)
    wide = up(pair_rows * MX, LANES)
    z_forward, y_forward, x_forward, x_back, y_back, z_back = tables(
        n_gx, n_gy, rows_x, rows_y, depth, pair_rows, group
    )
    spread = jnp.asarray(np.repeat(np.eye(channels), HALF, axis=0).astype(ml_dtypes.bfloat16))
    whole = pl.BlockSpec(memory_space=pltpu.VMEM)
    anywhere = pl.BlockSpec(memory_space=pl.ANY)
    limit = 60 * 2**20
    steps = fields // group
    weights = spectral_weight.reshape(pair_rows * MX, -1)
    weights = jnp.pad(weights, [(0, wide - pair_rows * MX), (0, 0)])
    state = plume_state.reshape(fields, cells_xy, depth)
    many = pltpu.SemaphoreType.DMA((slot // TILE, count))
    few = pltpu.SemaphoreType.DMA((n_gx,))
    chain = pltpu.SemaphoreType.DMA((n_gy, n_gx))
    cells, local = pl.pallas_call(
        functools.partial(modes_kernel, n_gx, n_gy, snapshots, channels, group),
        out_shape=(
            jax.ShapeDtypeStruct((fields * MZ, blocks * LANES), BF16),
            jax.ShapeDtypeStruct(state.shape, BF16),
        ),
        in_specs=[anywhere, whole, whole, anywhere, anywhere, anywhere, whole, whole],
        out_specs=(whole, anywhere),
        scratch_shapes=[
            pltpu.VMEM(state.shape, BF16),
            pltpu.VMEM(weights.shape, BF16),
            pltpu.VMEM(x_forward.shape, BF16),
            pltpu.VMEM(x_back.shape, BF16),
            pltpu.VMEM((blocks, slot * MZ, LANES), F32),
            pltpu.VMEM((count, slot, LANES), BF16),
            pltpu.VMEM((count, slot, LANES), BF16),
            pltpu.VMEM((count, slot, LANES), BF16),
            pltpu.VMEM((n_gx, slot, LANES), BF16),
            pltpu.VMEM((up(weights.shape[1], LANES), wide), F32),
            pltpu.VMEM((slot, 2 * wide), F32),
            pltpu.VMEM((slot, 2 * wide), F32),
            pltpu.VMEM((blocks, fields * MZ, LANES), F32),
            pltpu.VMEM(state.shape, BF16),
            pltpu.VMEM((channels * HALF, channels * HALF), BF16),
            pltpu.SemaphoreType.DMA((steps,)),
            pltpu.SemaphoreType.DMA((3,)),
            pltpu.SemaphoreType.DMA((snapshots,)),
            many, many, few, few, chain, chain,
        ],
        compiler_params=pltpu.CompilerParams(
            vmem_limit_bytes=limit, collective_id=0, has_side_effects=True
        ),
        name="modes",
    )(state, z_forward, y_forward, weights, x_forward, x_back, pointwise_weight, spread)

    slab = pl.BlockSpec((group, cells_xy, depth), lambda g: (g, 0, 0))
    result = pl.pallas_call(
        functools.partial(inverse_kernel, channels),
        grid=(steps,),
        out_shape=jax.ShapeDtypeStruct(state.shape, BF16),
        in_specs=[
            slab,
            pl.BlockSpec((group * MZ, blocks * LANES), lambda g: (g, 0)),
            whole,
            whole,
            pl.BlockSpec(memory_space=pltpu.SMEM),
        ],
        out_specs=slab,
        compiler_params=pltpu.CompilerParams(vmem_limit_bytes=limit),
        name="inverse",
    )(local, cells, y_back, z_back, channel_bias)
    return result.reshape(plume_state.shape)


def solution(mesh):
    placed = (P("groups", None, "gx", "gy", None), P("gy", "gx", None, None), P(), P())
    return jax.shard_map(
        functools.partial(body, mesh.shape["gx"], mesh.shape["gy"]),
        mesh=mesh,
        in_specs=placed,
        out_specs=P("groups", None, "gx", "gy", None),
        check_vma=False,
    )
```

```python
import functools
import math

import jax
import jax.numpy as jnp
import ml_dtypes
import numpy as np
from jax import lax
from jax.experimental import pallas as pl
from jax.experimental.pallas import tpu as pltpu
from jax.sharding import PartitionSpec as P

MX = 24
MY = 16
MZ = 16
LANES = 128
TILE = 16
HALF = 8
MESH = pl.DeviceIdType.MESH
F32 = jnp.float32
BF16 = jnp.bfloat16


def retained(kept, length):
    indices = np.arange(kept)
    return np.where(indices < kept // 2, indices, length - kept + indices)


def phases(freq_ids, positions, length):
    product = freq_ids[:, None] * positions[None, :] % length
    return np.float32(2.0 * math.pi / length) * product.astype(np.float32)


def forward_table(freq_ids, positions, length):
    angles = phases(freq_ids, positions, length).T
    cosine, sine = np.cos(angles), np.sin(angles)
    return np.stack([np.stack([cosine, -sine], 1), np.stack([sine, cosine], 1)], 1)


def inverse_table(freq_ids, positions, length):
    angles = phases(freq_ids, positions, length)
    cosine, sine = np.cos(angles), np.sin(angles)
    return np.stack([np.stack([cosine, sine], 1), np.stack([-sine, cosine], 1)], 0)


def up(value, step):
    return -(-value // step) * step


def pad_last(table, width):
    return np.pad(table, [(0, 0)] * (table.ndim - 1) + [(0, width - table.shape[-1])])


def tables(n_gx, n_gy, rows_x, rows_y, depth, pair_rows, group):
    length_x, length_y = n_gx * rows_x, n_gy * rows_y
    blocks = MY // pair_rows
    lanes_l = up(pair_rows * MX, LANES)
    angles = phases(np.arange(MZ), np.arange(depth), depth)
    z_forward = np.concatenate([np.cos(angles), -np.sin(angles)], 0)

    y_ids, x_ids = retained(MY, length_y), retained(MX, length_x)
    eye_x, eye_m = np.eye(rows_x), np.eye(pair_rows)
    fy = forward_table(y_ids, np.arange(length_y), length_y)
    fy = fy.reshape(n_gy, rows_y, 2, 2, blocks, pair_rows)
    y_forward = np.einsum("gypqbm,xw->gpxybwqm", fy, eye_x)
    y_forward = y_forward.reshape(n_gy, 2 * rows_x * rows_y, blocks, -1)
    y_forward = pad_last(y_forward, LANES).reshape(n_gy, 2 * rows_x * rows_y, blocks * LANES)

    fx = forward_table(x_ids, np.arange(length_x), length_x).reshape(n_gx, rows_x, 2, 2, MX)
    x_forward = np.einsum("ixqpk,mn->pnkixqm", fx, eye_m).reshape(2, pair_rows * MX, n_gx, -1)
    x_forward = pad_last(x_forward, LANES).reshape(2, pair_rows * MX, n_gx * LANES)
    x_forward = np.pad(x_forward, [(0, 0), (0, lanes_l - pair_rows * MX), (0, 0)])
    x_forward = x_forward.reshape(2 * lanes_l, n_gx * LANES).T

    ix = inverse_table(x_ids, np.arange(length_x), length_x).reshape(2, MX, 2, n_gx, rows_x)
    x_back = np.einsum("qkpix,mn->qnkixpm", ix, eye_m).reshape(2, pair_rows * MX, n_gx, -1)
    x_back = pad_last(x_back, LANES).reshape(2, pair_rows * MX, n_gx * LANES)
    x_back = np.pad(x_back, [(0, 0), (0, lanes_l - pair_rows * MX), (0, 0)])
    x_back = x_back.reshape(2 * lanes_l, n_gx * LANES)

    iy = inverse_table(y_ids, np.arange(length_y), length_y)
    iy = iy.reshape(2, blocks, pair_rows, 2, n_gy, rows_y)
    y_back = np.einsum("qbmpgy,xw->gpxybwqm", iy, eye_x)
    y_back = y_back.reshape(n_gy, 2, rows_x * rows_y, blocks, -1)
    y_back = pad_last(y_back, LANES).reshape(n_gy, 2, rows_x * rows_y, blocks * LANES)

    doubling = np.where(np.arange(MZ) == 0, 1.0, 2.0)[:, None]
    iz = np.stack([doubling * np.cos(angles), -doubling * np.sin(angles)], 0)
    iz = iz.astype(ml_dtypes.bfloat16).astype(np.float32) / (length_x * length_y * depth)
    z_back = np.einsum("pkz,jh->pjkhz", iz, np.eye(group))
    z_back = z_back.reshape(2 * group * MZ, group * depth)
    return [
        jnp.asarray(np.ascontiguousarray(t, dtype=np.float32).astype(ml_dtypes.bfloat16))
        for t in (z_forward, y_forward, x_forward, x_back, y_back, z_back)
    ]


def dot(a, b):
    return jnp.dot(a, b, preferred_element_type=F32)


def dot_lanes(a, b):
    return lax.dot_general(a, b, (((1,), (1,)), ((), ())), preferred_element_type=F32)


def each(count, one):
    if count <= 16:
        for s in range(1, count):
            one(s)
    else:
        lax.fori_loop(1, count, lambda s, _: (one(s), 0)[1], 0)


def modes_kernel(
    n_gx, n_gy, snapshots, channels, group,
    plume_in, z_forward, y_forward, weights_in, x_forward_in, x_back_in, pointwise, spread,
    out, local_out,
    plume, weights, x_forward, x_back, rows, sent,
    landed, back, going, mixers, pairs, mixed, order, local, kron,
    in_sem, table_sem, local_sem, send_one, recv_one, send_two, recv_two, send_on, recv_on,
):
    count = n_gx * n_gy
    my_x, my_y = lax.axis_index("gx"), lax.axis_index("gy")
    me = my_y * n_gx + my_x
    fields = snapshots * channels
    wide = mixers.shape[1]
    blocks = count // MZ
    slot_rows = sent.shape[1]
    steps = fields // group
    bands = [(at, min(2 * TILE, slot_rows - at)) for at in range(0, slot_rows, 2 * TILE)]
    parts_out = len(bands)

    def device(index):
        return {"gx": lax.rem(index, n_gx), "gy": lax.div(index, n_gx)}

    def chunk_in(g):
        part = pl.ds(g * group, group)
        return pltpu.make_async_copy(plume_in.at[part], plume.at[part], in_sem.at[g])

    for g in range(steps):
        chunk_in(g).start()
    held = [
        pltpu.make_async_copy(src, dst, table_sem.at[i])
        for i, (src, dst) in enumerate(
            [(weights_in, weights), (x_forward_in, x_forward), (x_back_in, x_back)]
        )
    ]
    for copy in held:
        copy.start()

    barrier = pltpu.get_barrier_semaphore()

    def greet(s):
        peer = lax.rem(me + s, count)
        pl.semaphore_signal(barrier, inc=1, device_id=device(peer), device_id_type=MESH)

    each(count, greet)
    size = channels * HALF
    scaled = dot_lanes(dot_lanes(spread[...], pointwise[...]).astype(BF16), spread[...])
    at_row = lax.broadcasted_iota(jnp.int32, (size, size), 0) % HALF
    at_column = lax.broadcasted_iota(jnp.int32, (size, size), 1) % HALF
    kron[...] = jnp.where(at_row == at_column, scaled, 0.0).astype(BF16)

    def first(s, at, part):
        peer = lax.rem(me + s, count)
        band = pl.ds(*bands[part])
        return pltpu.make_async_remote_copy(
            src_ref=sent.at[peer, band], dst_ref=landed.at[at, band],
            send_sem=send_one.at[part, s], recv_sem=recv_one.at[part, s],
            device_id=device(peer), device_id_type=MESH,
        )

    def send_part(part):
        band = pl.ds(*bands[part])
        for kz in range(MZ):
            for block in range(blocks):
                at, size = bands[part]
                taken = rows[block, pl.ds(at * MZ + kz, size, stride=MZ), :]
                sent[kz * blocks + block, band, :] = taken.astype(BF16)
        if part == 0:
            pl.semaphore_wait(barrier, count - 1)
        each(count, lambda s: first(s, me, part).start())

    def second(s, at):
        peer = lax.rem(my_x + s, n_gx)
        return pltpu.make_async_remote_copy(
            src_ref=going.at[peer], dst_ref=back.at[at],
            send_sem=send_two.at[s], recv_sem=recv_two.at[s],
            device_id={"gx": peer}, device_id_type=MESH,
        )

    def onward(h, s, owner_y):
        at = owner_y * n_gx + lax.rem(my_x + n_gx - s, n_gx)
        return pltpu.make_async_remote_copy(
            src_ref=back.at[at], dst_ref=back.at[at],
            send_sem=send_on.at[h, s], recv_sem=recv_on.at[h, s],
            device_id={"gy": lax.rem(my_y + h, n_gy)}, device_id_type=MESH,
        )

    def arrived(s):
        second(s, my_y * n_gx + lax.rem(my_x + n_gx - s, n_gx)).wait_recv()
        for h in range(1, n_gy):
            onward(h, s, my_y).start()

    def source(s):
        return lax.rem(me + count - s, count)

    rows[:, pl.ds(fields * MZ, (slot_rows - fields) * MZ), :] = jnp.zeros(
        (blocks, (slot_rows - fields) * MZ, LANES), F32
    )
    for g in range(steps):
        chunk_in(g).wait()
        parts = []
        for j in range(group):
            modes = dot_lanes(z_forward[...], plume[g * group + j]).astype(BF16)
            parts.append(jnp.concatenate([modes[:MZ], modes[MZ:]], axis=1))
        terms = dot(jnp.concatenate(parts, axis=0), y_forward[my_y])
        for block in range(blocks):
            rows[block, pl.ds(g * group * MZ, group * MZ), :] = terms[
                :, block * LANES : (block + 1) * LANES
            ]
        for part in range(parts_out):
            ready = min(-(-sum(bands[part]) // group), steps) - 1
            if ready == g:
                send_part(part)

    depth = plume.shape[2]

    def pointwise_of(t, piece=0, pieces=1):
        fld = pl.ds(t * channels, channels)

        def strip(i, _):
            base = pl.ds(pl.multiple_of(i * TILE, TILE), TILE)
            block = plume[fld, base, :].astype(F32)
            pair = jnp.concatenate(
                [block[:, h : h + HALF].reshape(size, depth) for h in (0, HALF)], axis=1
            )
            value = dot(kron[...], pair.astype(BF16))
            local[fld, base, :] = jnp.concatenate(
                [
                    value[:, h : h + depth].reshape(channels, HALF, depth)
                    for h in (0, depth)
                ],
                axis=1,
            ).astype(BF16)
            return 0

        strips = plume.shape[1] // TILE // pieces
        lax.fori_loop(piece * strips, (piece + 1) * strips, strip, 0, unroll=8)
        if piece == pieces - 1:
            local_copy(t).start()

    def local_copy(t):
        fld = pl.ds(t * channels, channels)
        return pltpu.make_async_copy(local.at[fld], local_out.at[fld], local_sem.at[t])

    landed[me] = sent[me]

    for copy in held:
        copy.wait()
    length = weights.shape[1]
    for at in range(0, length, LANES):
        width = min(LANES, length - at)
        chunk = weights[:, pl.ds(at, width)].astype(F32)
        if width < LANES:
            chunk = jnp.concatenate([chunk, jnp.zeros((wide, LANES - width), F32)], axis=1)
        mixers[pl.ds(at, LANES), :] = chunk.T
    pointwise_of(0)

    for part in range(parts_out):
        each(count, lambda s, part=part: first(s, source(s), part).wait_recv())
    summed = []
    for i in range(n_gx):
        total = landed[i].astype(F32)
        for g in range(1, n_gy):
            total += landed[g * n_gx + i].astype(F32)
        summed.append(total.astype(BF16))
    pairs[...] = dot(jnp.concatenate(summed, axis=1), x_forward[...]).astype(BF16).astype(F32)

    square = channels * channels
    mixed[...] = jnp.zeros_like(mixed)
    for t in range(snapshots):
        real = jnp.zeros((channels, wide), F32)
        imag = jnp.zeros((channels, wide), F32)
        for c in range(channels):
            mode_real = pairs[pl.ds(t * channels + c, 1), pl.ds(0, wide)]
            mode_imag = pairs[pl.ds(t * channels + c, 1), pl.ds(wide, wide)]
            weight_real = mixers[pl.ds(c * channels, channels), :]
            weight_imag = mixers[pl.ds(square + c * channels, channels), :]
            real += mode_real * weight_real - mode_imag * weight_imag
            imag += mode_real * weight_imag + mode_imag * weight_real
        mixed[pl.ds(t * channels, channels), pl.ds(0, wide)] = real
        mixed[pl.ds(t * channels, channels), pl.ds(wide, wide)] = imag
    cells = dot(mixed[...].astype(BF16), x_back[...]).astype(BF16)
    for i in range(n_gx):
        going[i] = cells[:, i * LANES : (i + 1) * LANES]

    each(n_gx, lambda s: second(s, me).start())
    back[me] = going[my_x]
    for h in range(1, n_gy):
        onward(h, 0, my_y).start()
    for t in range(1, snapshots):
        pointwise_of(t, 0, 2)
    each(n_gx, arrived)
    for t in range(1, snapshots):
        pointwise_of(t, 1, 2)
    for h in range(1, n_gy):
        owner_y = lax.rem(my_y + n_gy - h, n_gy)
        onward(h, 0, owner_y).wait_recv()
        each(n_gx, lambda s, h=h, owner_y=owner_y: onward(h, s, owner_y).wait_recv())
    for kz in range(MZ):
        for block in range(blocks):
            order[block, pl.ds(kz, fields, stride=MZ), :] = back[kz * blocks + block].astype(
                F32
            )[:fields]
    for block in range(blocks):
        out[:, pl.ds(block * LANES, LANES)] = order[block].astype(BF16)
    for part in range(parts_out):
        each(count, lambda s, part=part: first(s, me, part).wait_send())
    each(n_gx, lambda s: second(s, me).wait_send())
    for h in range(1, n_gy):
        onward(h, 0, my_y).wait_send()
        each(n_gx, lambda s, h=h: onward(h, s, my_y).wait_send())
    for t in range(snapshots):
        local_copy(t).wait()


def gelu(x):
    half = 0.5 * x
    return half + half * lax.erf(x * math.sqrt(0.5))


def inverse_kernel(channels, local, cells, y_back, z_back, bias, out):
    g = pl.program_id(0)
    half = lax.axis_index("gy")
    group, _, depth = local.shape
    both = jnp.concatenate(
        [dot_lanes(y_back[half, p], cells[...]).astype(BF16) for p in range(2)], axis=1
    )
    for j in range(0, group, 2):
        values = dot(both, z_back[:, j * depth : (j + 2) * depth])
        for h in range(2):
            level = bias[lax.rem(g * group + j + h, channels)]
            value = values[:, h * depth : (h + 1) * depth] + local[j + h].astype(F32) + level
            out[j + h] = gelu(value).astype(BF16)


def body(n_gx, n_gy, plume_state, spectral_weight, pointwise_weight, channel_bias):
    snapshots, channels, rows_x, rows_y, depth = plume_state.shape
    fields = snapshots * channels
    cells_xy = rows_x * rows_y
    pair_rows = spectral_weight.shape[1]
    count = n_gx * n_gy
    blocks = MY // pair_rows
    group = LANES // MZ
    slot = up(fields, TILE)
    wide = up(pair_rows * MX, LANES)
    z_forward, y_forward, x_forward, x_back, y_back, z_back = tables(
        n_gx, n_gy, rows_x, rows_y, depth, pair_rows, group
    )
    spread = jnp.asarray(np.repeat(np.eye(channels), HALF, axis=0).astype(ml_dtypes.bfloat16))
    whole = pl.BlockSpec(memory_space=pltpu.VMEM)
    anywhere = pl.BlockSpec(memory_space=pl.ANY)
    limit = 60 * 2**20
    steps = fields // group
    weights = spectral_weight.reshape(pair_rows * MX, -1)
    weights = jnp.pad(weights, [(0, wide - pair_rows * MX), (0, 0)])
    state = plume_state.reshape(fields, cells_xy, depth)
    many = pltpu.SemaphoreType.DMA((slot // TILE, count))
    few = pltpu.SemaphoreType.DMA((n_gx,))
    chain = pltpu.SemaphoreType.DMA((n_gy, n_gx))
    cells, local = pl.pallas_call(
        functools.partial(modes_kernel, n_gx, n_gy, snapshots, channels, group),
        out_shape=(
            jax.ShapeDtypeStruct((fields * MZ, blocks * LANES), BF16),
            jax.ShapeDtypeStruct(state.shape, BF16),
        ),
        in_specs=[anywhere, whole, whole, anywhere, anywhere, anywhere, whole, whole],
        out_specs=(whole, anywhere),
        scratch_shapes=[
            pltpu.VMEM(state.shape, BF16),
            pltpu.VMEM(weights.shape, BF16),
            pltpu.VMEM(x_forward.shape, BF16),
            pltpu.VMEM(x_back.shape, BF16),
            pltpu.VMEM((blocks, slot * MZ, LANES), F32),
            pltpu.VMEM((count, slot, LANES), BF16),
            pltpu.VMEM((count, slot, LANES), BF16),
            pltpu.VMEM((count, slot, LANES), BF16),
            pltpu.VMEM((n_gx, slot, LANES), BF16),
            pltpu.VMEM((up(weights.shape[1], LANES), wide), F32),
            pltpu.VMEM((slot, 2 * wide), F32),
            pltpu.VMEM((slot, 2 * wide), F32),
            pltpu.VMEM((blocks, fields * MZ, LANES), F32),
            pltpu.VMEM(state.shape, BF16),
            pltpu.VMEM((channels * HALF, channels * HALF), BF16),
            pltpu.SemaphoreType.DMA((steps,)),
            pltpu.SemaphoreType.DMA((3,)),
            pltpu.SemaphoreType.DMA((snapshots,)),
            many, many, few, few, chain, chain,
        ],
        compiler_params=pltpu.CompilerParams(
            vmem_limit_bytes=limit, collective_id=0, has_side_effects=True
        ),
        name="modes",
    )(state, z_forward, y_forward, weights, x_forward, x_back, pointwise_weight, spread)

    slab = pl.BlockSpec((group, cells_xy, depth), lambda g: (g, 0, 0))
    result = pl.pallas_call(
        functools.partial(inverse_kernel, channels),
        grid=(steps,),
        out_shape=jax.ShapeDtypeStruct(state.shape, BF16),
        in_specs=[
            slab,
            pl.BlockSpec((group * MZ, blocks * LANES), lambda g: (g, 0)),
            whole,
            whole,
            pl.BlockSpec(memory_space=pltpu.SMEM),
        ],
        out_specs=slab,
        compiler_params=pltpu.CompilerParams(vmem_limit_bytes=limit),
        name="inverse",
    )(local, cells, y_back, z_back, channel_bias)
    return result.reshape(plume_state.shape)


def solution(mesh):
    placed = (P("groups", None, "gx", "gy", None), P("gy", "gx", None, None), P(), P())
    return jax.shard_map(
        functools.partial(body, mesh.shape["gx"], mesh.shape["gy"]),
        mesh=mesh,
        in_specs=placed,
        out_specs=P("groups", None, "gx", "gy", None),
        check_vma=False,
    )
```
